128 devices in a mesh: site: 16 (over x, y), scen: 8 (over z, core).
Axes of the slice: x: 4, y: 4, z: 4, core: 2. Of those that a mesh axis runs over, the one named last changes fastest.
Arguments:
- normals: bfloat16 [40960, 2688], P('site', 'scen'), may hold values from -6 to 6
- pattern: int32 [64, 40], replicated, may hold values from 0 to 159, as said below
- factor: bfloat16 [64, 40, 256, 256], P('site', None, 'scen'), may hold values from -0.0625 to 0.0625
- temporal: bfloat16 [168, 168], replicated, may hold values from -0.5 to 0.5
- capacity: float32 [16384], P('site'), may hold values from 0.05 to 0.4
- spread: float32 [16384], P('site'), may hold values from 0.2 to 0.8
- bus_map: int32 [16384], replicated, may hold values from 0 to 1023
Outputs:
- bus_power: float32 [1024, 2688], P('site', 'scen')
The draws below stay inside these ranges and needn't reach their ends.
Inputs may be any that keep to these rules, and one draw needn't show every extreme that they name: `pattern`: each block row names 40 different column blocks. The 4 block rows of one index of site (rows k * 4 to (k + 1) * 4 - 1) name at most 5 different column blocks among those held by any one index of site (blocks j * 10 to (j + 1) * 10 - 1), and exactly 5 among those held by index k itself.
All inputs are finite; a program needn't handle non-finite values.
Results may differ from the reference program's by a relative error of at most 0.0013.
Values may be sent and summed in bfloat16 or wider, within the bound.
No kernel may reach another device: no remote copies, remote signals or barrier semaphores. Data moves between devices by JAX's collectives and lax.ppermute only.
A program may use at most 192 MiB of HBM per device.

```python
import math
import jax
import jax.numpy as jnp
from jax import lax

BLK = 256
HOURS = 168
NZ = 40
MAX_COLUMN_BLOCKS = 5
CB_DEV = 10
RB_DEV = 4
ROWS = 64
COLS = 160
SITES = 40960
SLAB = 16384
SCEN = 16
BUSES = 1024


def candidate_slots(sub_key):
    return jax.random.permutation(sub_key, CB_DEV)[:MAX_COLUMN_BLOCKS].astype(jnp.int32)


def draw_pattern(key, part):
    owning_devices = ROWS // RB_DEV
    key_perm, pairing_key, key_hub, key_row = jax.random.split(jax.random.fold_in(key, 11), 4)
    local_slots = jax.vmap(candidate_slots)(jax.random.split(key_perm, owning_devices * owning_devices)).reshape(owning_devices, owning_devices, MAX_COLUMN_BLOCKS)
    holder = jnp.arange(owning_devices, dtype=jnp.int32)
    cand_columns = holder[None, :, None] * CB_DEV + local_slots
    raw_gap = jnp.abs(holder[:, None] - holder[None, :])
    block_separation = jnp.minimum(raw_gap, owning_devices - raw_gap)
    pairing_reward = jax.random.randint(pairing_key, (owning_devices, owning_devices), 0, 2048, dtype=jnp.int32) // (1 + block_separation)
    central_marker = jax.random.randint(key_hub, (owning_devices,), 0, 4, dtype=jnp.int32) == 0
    central_reward = jnp.where(central_marker, 1024, 0).astype(jnp.int32)
    ownership_reward = jnp.where(block_separation == 0, 100000, 0).astype(jnp.int32)
    device_reward = pairing_reward + central_reward[None, :] + ownership_reward
    row_holder_device = jnp.arange(ROWS, dtype=jnp.int32) // RB_DEV
    row_jitter = jax.random.randint(key_row, (ROWS, owning_devices, MAX_COLUMN_BLOCKS), 0, 1024, dtype=jnp.int32)
    tiebreak_jitter = jnp.arange(owning_devices * MAX_COLUMN_BLOCKS, dtype=jnp.int32).reshape(owning_devices, MAX_COLUMN_BLOCKS)
    placement_scores = (device_reward[row_holder_device][:, :, None] + row_jitter) * (owning_devices * MAX_COLUMN_BLOCKS) + tiebreak_jitter[None, :, :]
    chosen = lax.top_k(placement_scores.reshape(ROWS, owning_devices * MAX_COLUMN_BLOCKS), NZ)[1]
    row_cands = cand_columns[row_holder_device].reshape(ROWS, owning_devices * MAX_COLUMN_BLOCKS)
    return jnp.take_along_axis(row_cands, chosen, axis=1).astype(jnp.int32)


def touch_ends(result, stream_key, smallest, largest):
    index_at = [jax.random.randint(jax.random.fold_in(stream_key, axis), (), 0, length) for axis, length in enumerate(result.shape)]
    longest = result.shape.index(max(result.shape))
    next_to = index_at[:longest] + [(index_at[longest] + 1) % result.shape[longest]] + index_at[longest + 1:]
    return result.at[tuple(index_at)].set(smallest).at[tuple(next_to)].set(largest)


def level_of(stream_key, shape, cuts, least, high):
    gain, own = 1.0, jax.random.fold_in(stream_key, 6)
    for position, parts in cuts:
        draws = jnp.exp(jax.random.uniform(jax.random.fold_in(own, position), (parts,), jnp.float32, least / len(cuts), high / len(cuts)))
        gain = gain * jnp.repeat(draws, shape[position] // parts).reshape([-1 if axis == position else 1 for axis in range(len(shape))])
    return gain


def gaussian(own_key, dims, scale, bound, cuts=(), kind=jnp.bfloat16):
    result = scale * jax.random.normal(own_key, dims, jnp.float32)
    if cuts:
        result = result * level_of(own_key, dims, cuts, -0.22, 0.18)
    return jnp.clip(result, -bound, bound).astype(kind)


def setup_inputs(seed: int = 0) -> dict:
    splits = jax.random.split(jax.random.key(seed), 8)
    return {
        "normals": gaussian(splits[0], (SITES, SCEN * HOURS), 1.0, 6.0, ((0, 16), (1, 8))),
        "pattern": draw_pattern(jax.random.fold_in(splits[7], 71), 0),
        "factor": gaussian(splits[2], (ROWS, NZ, BLK, BLK), (NZ * BLK) ** -0.5, 0.0625, ((0, 16), (2, 8))),
        "temporal": gaussian(splits[3], (HOURS, HOURS), HOURS ** -0.5, 0.5),
        "capacity": jnp.clip(jnp.exp(math.log(0.4) - 2.0794415 * jax.random.uniform(splits[4], (SLAB,), jnp.float32) ** level_of(splits[4], (SLAB,), ((0, 16),), -0.2, 0.2)), 0.05, 0.4),
        "spread": jnp.clip(jnp.exp(math.log(0.8) - 1.3862944 * jax.random.uniform(splits[5], (SLAB,), jnp.float32) ** level_of(splits[5], (SLAB,), ((0, 16),), -0.2, 0.2)), 0.2, 0.8),
        "bus_map": touch_ends(jax.random.randint(splits[6], (SLAB,), 0, BUSES), jax.random.fold_in(splits[6], 1), 0, BUSES - 1).astype(jnp.int32),
    }


def reference(normals, pattern, factor, temporal, capacity, spread, bus_map):
    row_width = SCEN * HOURS
    blocks = normals.reshape(COLS, BLK, row_width)

    def one_block_row(inputs):
        columns, factor_row = inputs
        picked = jnp.take(blocks, columns.astype(jnp.int32), axis=0)
        spatial = jnp.einsum("tij,tjw->iw", factor_row.astype(jnp.float32), picked.astype(jnp.float32))
        return spatial.astype(jnp.bfloat16)

    spatial = lax.map(one_block_row, (pattern, factor))
    hourly = spatial.reshape(SLAB, SCEN, HOURS).astype(jnp.float32)
    weather = jnp.einsum("nsg,hg->nsh", hourly, temporal.astype(jnp.float32))
    scale_rows = capacity[:, None, None]
    spread_rows = spread[:, None, None]
    injected = (scale_rows * jnp.exp(spread_rows * weather - 0.5 * spread_rows * spread_rows)).astype(jnp.bfloat16)
    injected = injected.reshape(SLAB, row_width).astype(jnp.float32)
    return jax.ops.segment_sum(injected, bus_map.astype(jnp.int32), num_segments=BUSES)
```

```python
import functools

import jax
import jax.numpy as jnp
from jax import lax
from jax.experimental import pallas as pl
from jax.experimental.pallas import tpu as pltpu
from jax.sharding import PartitionSpec as P

BLK = 256
HALF = 128
HOURS = 168
NZ = 40
SLOTS = 5
RB_DEV = 4
CB_DEV = 10
SIDE = 4
CHUNK = 10
BUSES = 1024


def shift(value, dx, dy):
    n = SIDE
    pairs = [
        (x * n + y, ((x + dx) % n) * n + (y + dy) % n) for x in range(n) for y in range(n)
    ]
    return lax.ppermute(value, "site", pairs)


def step(value, axis, d):
    return shift(value, d, 0) if axis == 0 else shift(value, 0, d)


def transpose_kernel(z_ref, lo_ref, hi_ref):
    z = z_ref[...].T
    lo_ref[0] = z[:, :HALF]
    hi_ref[0] = z[:, HALF:]


def transposed(normals):
    blocks = normals.shape[0] // BLK
    width = normals.shape[1]
    out = jax.ShapeDtypeStruct((blocks, width, HALF), normals.dtype)
    spec = pl.BlockSpec((1, width, HALF), lambda b: (b, 0, 0))
    return pl.pallas_call(
        transpose_kernel,
        grid=(blocks,),
        in_specs=[pl.BlockSpec((BLK, width), lambda b: (b, 0))],
        out_specs=[spec, spec],
        out_shape=[out, out],
    )(normals)


def slots_of(ex, ey):
    return (ex * SIDE + ey) * SLOTS


def main_kernel(
    slot_ref, own_ref, *refs
):
    (lo_line, hi_line, lo_p, lo_q, hi_p, hi_q) = (
        refs[0:4], refs[4:8], refs[8:11], refs[11:14], refs[14:17], refs[17:20]
    )
    f_ref, temporal_ref, cap_ref, spr_ref, bus_ref, out_ref, zlo, zhi, acc, power, sem = refs[20:]
    r, c = pl.program_id(0), pl.program_id(1)

    def copies(fn):
        for ex in range(SIDE):
            for ey in range(SIDE):
                base = slots_of(ex, ey)
                for s in range(SLOTS):
                    local = own_ref[base + s]
                    if ey == 0:
                        src = lo_line[ex].at[local]
                    elif ex == 0:
                        src = lo_p[SIDE - 1 - ey].at[s]
                    else:
                        src = lo_q[SIDE - 1 - ey].at[(ex - 1) * SLOTS + s]
                    fn(pltpu.make_async_copy(src, zlo.at[base + s], sem))
                    if ex == 0:
                        src = hi_line[ey].at[local]
                    elif ey == 0:
                        src = hi_p[SIDE - 1 - ex].at[s]
                    else:
                        src = hi_q[SIDE - 1 - ex].at[(ey - 1) * SLOTS + s]
                    fn(pltpu.make_async_copy(src, zhi.at[base + s], sem))

    @pl.when((r == 0) & (c == 0))
    def _():
        copies(lambda d: d.start())
        power[...] = jnp.zeros_like(power)
        copies(lambda d: d.wait())

    @pl.when(c == 0)
    def _():
        acc[...] = jnp.zeros_like(acc)

    total = acc[...]
    for tt in range(CHUNK):
        slot = slot_ref[r * NZ + c * CHUNK + tt]
        z = jnp.concatenate([zlo[slot], zhi[slot]], axis=1)
        total += lax.dot_general(
            z, f_ref[0, tt], (((1,), (1,)), ((), ())), preferred_element_type=jnp.float32
        )
    acc[...] = total

    @pl.when(c == pl.num_programs(1) - 1)
    def _():
        cap, spr = cap_ref[0], spr_ref[0]
        parts = []
        for s in range(acc.shape[0] // HOURS):
            sp = acc[s * HOURS : (s + 1) * HOURS, :].astype(jnp.bfloat16)
            w = jnp.dot(temporal_ref[...], sp, preferred_element_type=jnp.float32)
            parts.append(cap * jnp.exp(spr * w - 0.5 * spr * spr))
        inj = jnp.concatenate(parts, axis=0).astype(jnp.bfloat16)
        buses = lax.broadcasted_iota(jnp.int32, (BUSES, BLK), 0)
        onehot = jnp.where(buses == bus_ref[0], 1.0, 0.0).astype(jnp.bfloat16)
        power[...] += lax.dot_general(
            onehot, inj, (((1,), (1,)), ((), ())), preferred_element_type=jnp.float32
        )

    @pl.when((c == pl.num_programs(1) - 1) & (r == pl.num_programs(0) - 1))
    def _():
        out_ref[...] = power[...].astype(jnp.bfloat16)


def main(slots, own, arrays, factor, temporal, cap, spr, bus, width):
    any_spec = pl.BlockSpec(memory_space=pl.ANY)
    vec = pl.BlockSpec((1, 1, BLK), lambda r, c, *_: (r, 0, 0))
    grid_spec = pltpu.PrefetchScalarGridSpec(
        num_scalar_prefetch=2,
        grid=(RB_DEV, NZ // CHUNK),
        in_specs=[any_spec] * len(arrays)
        + [
            pl.BlockSpec((1, CHUNK, BLK, BLK), lambda r, c, *_: (r, c, 0, 0)),
            pl.BlockSpec((HOURS, HOURS), lambda r, c, *_: (0, 0)),
            vec,
            vec,
            vec,
        ],
        out_specs=pl.BlockSpec((BUSES, width), lambda r, c, *_: (0, 0)),
        scratch_shapes=[
            pltpu.VMEM((SIDE * SIDE * SLOTS, width, HALF), jnp.bfloat16),
            pltpu.VMEM((SIDE * SIDE * SLOTS, width, HALF), jnp.bfloat16),
            pltpu.VMEM((width, BLK), jnp.float32),
            pltpu.VMEM((BUSES, width), jnp.float32),
            pltpu.SemaphoreType.DMA,
        ],
    )
    return pl.pallas_call(
        main_kernel,
        grid_spec=grid_spec,
        out_shape=jax.ShapeDtypeStruct((BUSES, width), jnp.bfloat16),
        compiler_params=pltpu.CompilerParams(vmem_limit_bytes=48 << 20),
    )(slots, own, *arrays, factor, temporal, cap, spr, bus)


def shards(normals, pattern, factor, temporal, capacity, spread, bus_map):
    width = normals.shape[1]
    n = SIDE
    sites = n * n
    me = lax.axis_index("site")
    x, y = me // n, me % n
    portion = lax.all_gather(factor, "scen", axis=2, tiled=True)

    ids = jnp.arange(sites * CB_DEV, dtype=jnp.int32)
    wanted = pattern.reshape(sites, -1)
    needed = jnp.any(wanted[:, :, None] == ids[None, None, :], axis=1)
    needed = needed.reshape(sites, sites, CB_DEV).astype(jnp.int32)
    lower = (jnp.arange(CB_DEV)[:, None] < jnp.arange(CB_DEV)[None, :]).astype(jnp.int32)
    rank = jnp.sum(needed[:, :, :, None] * lower[None, None], axis=2)
    slot_ids = jnp.arange(SLOTS, dtype=jnp.int32)
    chosen = (needed[..., None] == 1) & (rank[..., None] == slot_ids)
    local_ids = jnp.arange(CB_DEV, dtype=jnp.int32)
    table = jnp.sum(jnp.where(chosen, local_ids[:, None], 0), axis=2)

    def at(ex, ey):
        return ((x + ex) % n) * n + (y + ey) % n

    def picks(user, holders):
        return jnp.concatenate([table[user, h] for h in holders])

    lo, hi = transposed(normals)
    line = []
    for axis, own in ((0, lo), (1, hi)):
        below = step(own, axis, 1)
        above = step(own, axis, -1)
        line.append([own, above, None, below])
    for axis in (0, 1):
        _, above, _, below = line[axis]
        half = CB_DEV // 2
        far = [step(below[:half], axis, 1), step(above[half:], axis, -1)]
        line[axis][2] = jnp.concatenate(far, axis=0)
    near, rest = [], []
    for axis in (0, 1):
        near.append([])
        rest.append([])
        for d in range(1, n):
            user = at(0, d) if axis == 0 else at(d, 0)
            holders = [at(e, 0) if axis == 0 else at(0, e) for e in range(n)]
            p = jnp.take(line[axis][0], table[user, holders[0]], axis=0)
            near[axis].append(step(p, 1 - axis, d))
            q = jnp.concatenate(
                [jnp.take(line[axis][e], table[user, holders[e]], axis=0) for e in range(1, n)]
            )
            rest[axis].append(step(q, 1 - axis, d))

    own = jnp.concatenate([table[me, at(ex, ey)] for ex in range(n) for ey in range(n)])
    cols = lax.dynamic_slice_in_dim(pattern, me * RB_DEV, RB_DEV, 0).reshape(-1)
    holder = cols // CB_DEV
    ex = (holder // n - x) % n
    ey = (holder % n - y) % n
    my_rank = lax.dynamic_index_in_dim(rank, me, 0, keepdims=False).reshape(-1)
    slots = (ex * n + ey) * SLOTS + my_rank[cols]
    arrays = line[0] + line[1] + near[0] + rest[0] + near[1] + rest[1]
    rows = RB_DEV * BLK
    bus = lax.dynamic_slice_in_dim(bus_map, me * rows, rows, 0)
    shape = (RB_DEV, 1, BLK)
    power = main(
        slots, own, arrays, portion, temporal,
        capacity.reshape(shape), spread.reshape(shape), bus.reshape(shape), width,
    )
    tiles = lax.all_to_all(power.reshape(sites, -1, width), "site", 0, 0, tiled=True)
    return jnp.sum(tiles.astype(jnp.float32), axis=0)


def solution(mesh):
    placed = (P("site", "scen"), P(), P("site", None, "scen", None), P(), P("site"), P("site"), P())
    return jax.shard_map(
        shards, mesh=mesh, in_specs=placed, out_specs=P("site", "scen"), check_vma=False
    )
```

```python
import functools

import jax
import jax.numpy as jnp
from jax import lax
from jax.experimental import pallas as pl
from jax.experimental.pallas import tpu as pltpu
from jax.sharding import PartitionSpec as P

BLK = 256
HALF = 128
HOURS = 168
NZ = 40
SLOTS = 5
RB_DEV = 4
CB_DEV = 10
SIDE = 4
BUSES = 1024
COLS = 160


def shift(value, dx, dy):
    n = SIDE
    pairs = [
        (x * n + y, ((x + dx) % n) * n + (y + dy) % n) for x in range(n) for y in range(n)
    ]
    return lax.ppermute(value, "site", pairs)


def step(value, axis, d):
    return shift(value, d, 0) if axis == 0 else shift(value, 0, d)


def wait_all(copies):
    for c in copies:
        c.start()
    for c in copies:
        c.wait()


def after(value, *others):
    return lax.optimization_barrier((value, *others))[0]


def reblock_kernel(z_ref, lo_ref, hi_ref, sem):
    copies = []
    for b in range(CB_DEV):
        for h, out in enumerate((lo_ref, hi_ref)):
            src = z_ref.at[:, pl.ds(b * BLK + h * HALF, HALF)]
            copies.append(pltpu.make_async_copy(src, out.at[b], sem))
    wait_all(copies)


def reblocked(normals_t):
    width = normals_t.shape[0]
    out = jax.ShapeDtypeStruct((CB_DEV, width, HALF), normals_t.dtype)
    any_spec = pl.BlockSpec(memory_space=pl.ANY)
    return pl.pallas_call(
        reblock_kernel,
        in_specs=[any_spec],
        out_specs=[pl.BlockSpec(memory_space=pltpu.VMEM)] * 2,
        out_shape=[out, out],
        scratch_shapes=[pltpu.SemaphoreType.DMA],
    )(normals_t)


def device_at(x, y, ex, ey):
    return lax.rem(x + ex, SIDE) * SIDE + lax.rem(y + ey, SIDE)


def pick_kernel(hops, holders, me_ref, table_ref, *refs):
    count = len(holders)
    lines, outs, sem = (refs[:count], refs[count : 2 * count]), refs[2 * count : -1], refs[-1]
    x, y = me_ref[0] // SIDE, lax.rem(me_ref[0], SIDE)
    copies = []
    for axis in (0, 1):
        for k, d in enumerate(hops):
            user = device_at(x, y, 0, d) if axis == 0 else device_at(x, y, d, 0)
            out = outs[axis * len(hops) + k]
            for i, e in enumerate(holders):
                holder = device_at(x, y, e, 0) if axis == 0 else device_at(x, y, 0, e)
                for s in range(SLOTS):
                    local = table_ref[(user * SIDE * SIDE + holder) * SLOTS + s]
                    src = lines[axis][i].at[local]
                    copies.append(pltpu.make_async_copy(src, out.at[i * SLOTS + s], sem))
    wait_all(copies)


def picked(hops, holders, scalars, lines):
    width = lines[0][0].shape[1]
    out = jax.ShapeDtypeStruct((len(holders) * SLOTS, width, HALF), lines[0][0].dtype)
    outs = 2 * len(hops)
    return pl.pallas_call(
        functools.partial(pick_kernel, hops, holders),
        grid_spec=pltpu.PrefetchScalarGridSpec(
            num_scalar_prefetch=2,
            grid=(),
            in_specs=[pl.BlockSpec(memory_space=pl.ANY)] * (2 * len(holders)),
            out_specs=[pl.BlockSpec(memory_space=pltpu.VMEM)] * outs,
            scratch_shapes=[pltpu.SemaphoreType.DMA],
        ),
        out_shape=[out] * outs,
        compiler_params=pltpu.CompilerParams(vmem_limit_bytes=32 << 20),
    )(*scalars, *[lines[axis][e] for axis in (0, 1) for e in holders])


def slots_of(ex, ey):
    return (ex * SIDE + ey) * SLOTS


def main_kernel(me_ref, table_ref, rank_ref, cols_ref, *refs):
    lo_line, hi_line = refs[0:4], refs[4:8]
    sent = {(0, 1): refs[8], (0, 3): refs[9], (1, 1): refs[10], (1, 3): refs[11]}
    last = {(0, 1): refs[12], (0, 3): refs[13], (1, 1): refs[14], (1, 3): refs[15]}
    opposite = refs[16:18]
    f_ref, temporal_ref, cap_ref, spr_ref, bus_ref, out_ref, zlo, zhi, power, sem = refs[18:]

    def arrived(axis, d, e, s):
        if d == 2:
            return opposite[axis].at[e * SLOTS + s]
        if e == 2:
            return last[axis, d].at[s]
        return sent[axis, d].at[(e - e // 3) * SLOTS + s]

    r = pl.program_id(0)
    me = me_ref[0]
    x, y = me // SIDE, lax.rem(me, SIDE)

    def slot_at(t):
        col = cols_ref[(me * RB_DEV + r) * NZ + t]
        holder = col // CB_DEV
        ex = lax.rem(holder // SIDE - x + SIDE, SIDE)
        ey = lax.rem(lax.rem(holder, SIDE) - y + SIDE, SIDE)
        return slots_of(ex, ey) + rank_ref[me * COLS + col]

    def copies(fn):
        for ex in range(SIDE):
            for ey in range(SIDE):
                base = slots_of(ex, ey)
                holder = device_at(x, y, ex, ey)
                for s in range(SLOTS):
                    local = table_ref[(me * SIDE * SIDE + holder) * SLOTS + s]
                    if ey == 0:
                        src = lo_line[ex].at[local]
                    else:
                        src = arrived(0, SIDE - ey, ex, s)
                    fn(pltpu.make_async_copy(src, zlo.at[base + s], sem))
                    if ex == 0:
                        src = hi_line[ey].at[local]
                    else:
                        src = arrived(1, SIDE - ex, ey, s)
                    fn(pltpu.make_async_copy(src, zhi.at[base + s], sem))

    @pl.when(r == 0)
    def _():
        copies(lambda d: d.start())
        power[...] = jnp.zeros_like(power)
        copies(lambda d: d.wait())

    total = None
    for t in range(NZ):
        slot = slot_at(t)
        z = jnp.concatenate([zlo[slot], zhi[slot]], axis=1)
        term = lax.dot_general(
            z, f_ref[0, t], (((1,), (1,)), ((), ())), preferred_element_type=jnp.float32
        )
        total = term if total is None else total + term
    cap, spr = cap_ref[0], spr_ref[0]
    parts = []
    for s in range(total.shape[0] // HOURS):
        spatial = total[s * HOURS : (s + 1) * HOURS].astype(jnp.bfloat16)
        weather = jnp.dot(temporal_ref[...], spatial, preferred_element_type=jnp.float32)
        parts.append(cap * jnp.exp(spr * weather - 0.5 * spr * spr))
    injected = jnp.concatenate(parts, axis=0).astype(jnp.bfloat16)
    buses = lax.broadcasted_iota(jnp.int32, (BUSES, BLK), 0)
    onehot = jnp.where(buses == bus_ref[0], 1.0, 0.0).astype(jnp.bfloat16)
    power[...] += lax.dot_general(
        onehot, injected, (((1,), (1,)), ((), ())), preferred_element_type=jnp.float32
    )

    @pl.when(r == pl.num_programs(0) - 1)
    def _():
        out_ref[...] = power[...].astype(jnp.bfloat16)


def main(scalars, arrays, factor, temporal, cap, spr, bus, width):
    any_spec = pl.BlockSpec(memory_space=pltpu.HBM)
    vec = pl.BlockSpec((1, 1, BLK), lambda r, *_: (r, 0, 0))
    grid_spec = pltpu.PrefetchScalarGridSpec(
        num_scalar_prefetch=len(scalars),
        grid=(RB_DEV,),
        in_specs=[any_spec] * len(arrays)
        + [
            pl.BlockSpec((1, NZ, BLK, BLK), lambda r, *_: (r, 0, 0, 0)),
            pl.BlockSpec((HOURS, HOURS), lambda r, *_: (0, 0)),
            vec,
            vec,
            vec,
        ],
        out_specs=pl.BlockSpec((BUSES, width), lambda r, *_: (0, 0)),
        scratch_shapes=[
            pltpu.VMEM((SIDE * SIDE * SLOTS, width, HALF), jnp.bfloat16),
            pltpu.VMEM((SIDE * SIDE * SLOTS, width, HALF), jnp.bfloat16),
            pltpu.VMEM((BUSES, width), jnp.float32),
            pltpu.SemaphoreType.DMA,
        ],
    )
    return pl.pallas_call(
        main_kernel,
        grid_spec=grid_spec,
        out_shape=jax.ShapeDtypeStruct((BUSES, width), jnp.bfloat16),
        compiler_params=pltpu.CompilerParams(vmem_limit_bytes=48 << 20),
        cost_estimate=pl.CostEstimate(
            flops=2 * RB_DEV * NZ * BLK * BLK * width,
            bytes_accessed=36 << 20,
            transcendentals=RB_DEV * BLK * width,
        ),
    )(*scalars, *arrays, factor, temporal, cap, spr, bus)


def shards(normals, pattern, factor, temporal, capacity, spread, bus_map):
    width = normals.shape[1]
    n = SIDE
    sites = n * n
    me = lax.axis_index("site")
    portion = lax.all_gather(factor, "scen", axis=2, tiled=True)

    ids = jnp.arange(sites * CB_DEV, dtype=jnp.int32)
    wanted = pattern.reshape(sites, -1)
    needed = jnp.any(wanted[:, :, None] == ids[None, None, :], axis=1)
    needed = needed.reshape(sites, sites, CB_DEV).astype(jnp.int32)
    lower = (jnp.arange(CB_DEV)[:, None] < jnp.arange(CB_DEV)[None, :]).astype(jnp.int32)
    rank = jnp.sum(needed[:, :, :, None] * lower[None, None], axis=2)
    slot_ids = jnp.arange(SLOTS, dtype=jnp.int32)
    chosen = (needed[..., None] == 1) & (rank[..., None] == slot_ids)
    local_ids = jnp.arange(CB_DEV, dtype=jnp.int32)
    table = jnp.sum(jnp.where(chosen, local_ids[:, None], 0), axis=2)

    table = table.reshape(-1)
    index = me.reshape(1).astype(jnp.int32)

    lo, hi = reblocked(normals.T)
    lines = [[lo, None, None, None], [hi, None, None, None]]
    ring = [(axis, e) for axis in (0, 1) for e in (1, 3)]
    for axis, e in ring:
        lines[axis][e] = step(lines[axis][0], axis, -e)
    first = [lines[axis][e] for axis, e in ring]
    lines[0][2] = step(after(lo, *first), 0, 2)
    lines[1][2] = step(after(hi, *first), 1, 2)
    second = [lines[0][2], lines[1][2]]
    tables = (index, table)
    out = picked((1, 3), (0, 1, 3), tables, lines)
    sent = [step(after(b, *second), 1 - axis, d) for b, (axis, d) in zip(out, ring)]
    out = picked((2,), (0, 1, 2, 3), tables, lines)
    opposite = [step(after(b, *sent), 1 - axis, 2) for axis, b in enumerate(out)]
    out = picked((1, 3), (2,), tables, lines)
    last = [step(after(b, *opposite), 1 - axis, d) for b, (axis, d) in zip(out, ring)]
    arrays = lines[0] + lines[1] + sent + last + opposite
    scalars = (index, table, rank.reshape(-1), pattern.reshape(-1))
    rows = RB_DEV * BLK
    bus = lax.dynamic_slice_in_dim(bus_map, me * rows, rows, 0)
    shape = (RB_DEV, 1, BLK)
    power = main(
        scalars, arrays, portion, temporal,
        capacity.reshape(shape), spread.reshape(shape), bus.reshape(shape), width,
    )
    tiles = lax.all_to_all(power.reshape(sites, -1, width), "site", 0, 0, tiled=True)
    return jnp.sum(tiles.astype(jnp.float32), axis=0)


def solution(mesh):
    placed = (P("site", "scen"), P(), P("site", None, "scen", None), P(), P("site"), P("site"), P())
    return jax.shard_map(
        shards, mesh=mesh, in_specs=placed, out_specs=P("site", "scen"), check_vma=False
    )
```

```python
import functools

import jax
import jax.numpy as jnp
from jax import lax
from jax.experimental import pallas as pl
from jax.experimental.pallas import tpu as pltpu
from jax.sharding import PartitionSpec as P

BLK = 256
HALF = 128
HOURS = 168
NZ = 40
SLOTS = 5
FEW = 5
RB_DEV = 4
CB_DEV = 10
SIDE = 4
BUSES = 1024
COLS = 160
ALL_VMEM = 60 << 20


def shift(value, dx, dy):
    n = SIDE
    pairs = [
        (x * n + y, ((x + dx) % n) * n + (y + dy) % n) for x in range(n) for y in range(n)
    ]
    return lax.ppermute(value, "site", pairs)


def step(value, axis, d):
    return shift(value, d, 0) if axis == 0 else shift(value, 0, d)


def after(value, *others):
    return lax.optimization_barrier((value, *others))[0]


VMEM = pl.BlockSpec(memory_space=pltpu.VMEM)


def reblock_kernel(z_ref, *outs):
    for b in range(CB_DEV):
        for h in range(2):
            start = b * BLK + h * HALF
            outs[h * 2 + b // FEW][b % FEW] = z_ref[:, start : start + HALF]


def reblocked(normals_t):
    width = normals_t.shape[0]
    out = jax.ShapeDtypeStruct((FEW, width, HALF), normals_t.dtype)
    return pl.pallas_call(
        reblock_kernel,
        in_specs=[VMEM],
        out_specs=[VMEM] * 4,
        out_shape=[out] * 4,
        compiler_params=pltpu.CompilerParams(vmem_limit_bytes=ALL_VMEM),
    )(normals_t)


ANY = pl.BlockSpec(memory_space=pl.ANY)


def start_block(pair, local, target, sem):
    @pl.when(local < FEW)
    def _():
        pltpu.make_async_copy(pair[0].at[jnp.minimum(local, FEW - 1)], target, sem).start()

    @pl.when(local >= FEW)
    def _():
        pltpu.make_async_copy(pair[1].at[jnp.maximum(local - FEW, 0)], target, sem).start()


def wait_block(pair, target, sem):
    pltpu.make_async_copy(pair[0].at[0], target, sem).wait()


def pairs(refs):
    return [refs[k : k + 2] for k in range(0, len(refs), 2)]


def device_at(x, y, ex, ey):
    return lax.rem(x + ex, SIDE) * SIDE + lax.rem(y + ey, SIDE)


def pick_kernel(hops, holders, aliased, me_ref, table_ref, *refs):
    span, count = len(holders), 2 * len(hops)
    held = pairs(refs[: 4 * span])
    refs = refs[4 * span + aliased * count :]
    outs, buffers, came, gone = refs[:count], *refs[count:]
    x, y = me_ref[0] // SIDE, lax.rem(me_ref[0], SIDE)
    for k in range(count):
        axis, d = k // len(hops), hops[k % len(hops)]
        user = device_at(x, y, 0, d) if axis == 0 else device_at(x, y, d, 0)
        for i, e in enumerate(holders):
            holder = device_at(x, y, e, 0) if axis == 0 else device_at(x, y, 0, e)
            for s in range(SLOTS):
                local = table_ref[(user * SIDE * SIDE + holder) * SLOTS + s]
                start_block(held[axis * span + i], local, buffers.at[k, i, s], came.at[k])
    for k in range(count):
        for i in range(span):
            pltpu.make_async_copy(held[0][0], buffers.at[k, i], came.at[k]).wait()
        for i, e in enumerate(holders):
            target = outs[k].at[pl.ds(e * SLOTS, SLOTS)]
            pltpu.make_async_copy(buffers.at[k, i], target, gone.at[k, i]).start()
    for k in range(count):
        for i, e in enumerate(holders):
            target = outs[k].at[pl.ds(e * SLOTS, SLOTS)]
            pltpu.make_async_copy(buffers.at[k, i], target, gone.at[k, i]).wait()


def picked(hops, holders, scalars, lines, begun=()):
    width = lines[0][0][0].shape[1]
    out = jax.ShapeDtypeStruct((SIDE * SLOTS, width, HALF), jnp.bfloat16)
    outs, span = 2 * len(hops), len(holders)
    held = [p for line in lines for e in holders for p in line[e]]
    return pl.pallas_call(
        functools.partial(pick_kernel, hops, holders, bool(begun)),
        grid_spec=pltpu.PrefetchScalarGridSpec(
            num_scalar_prefetch=2,
            grid=(),
            in_specs=[ANY] * (len(held) + len(begun)),
            out_specs=[ANY] * outs,
            scratch_shapes=[
                pltpu.VMEM((outs, span, SLOTS, width, HALF), out.dtype),
                pltpu.SemaphoreType.DMA((outs,)),
                pltpu.SemaphoreType.DMA((outs, span)),
            ],
        ),
        out_shape=[out] * outs,
        input_output_aliases={2 + len(held) + k: k for k in range(len(begun))},
        compiler_params=pltpu.CompilerParams(vmem_limit_bytes=ALL_VMEM),
    )(*scalars, *held, *begun)


def slots_of(ex, ey):
    return (ex * SIDE + ey) * SLOTS


NT = (((1,), (1,)), ((), ()))


def early_kernel(me_ref, table_ref, rank_ref, cols_ref, *refs):
    held, sent, f_ref, bus_ref, acc_ref, use_ref, onehot_ref, zlo, zhi, sem = (
        pairs(refs[:16]), refs[16:20], *refs[20:]
    )
    r = pl.program_id(0)
    me = me_ref[0]
    x, y = me // SIDE, lax.rem(me, SIDE)

    def slot_at(t):
        col = cols_ref[(me * RB_DEV + r) * NZ + t]
        holder = col // CB_DEV
        ex = lax.rem(holder // SIDE - x + SIDE, SIDE)
        ey = lax.rem(lax.rem(holder, SIDE) - y + SIDE, SIDE)
        return slots_of(ex, ey) + rank_ref[me * COLS + col]

    @pl.when(r == 0)
    def _():
        for axis, z in ((0, zlo), (1, zhi)):
            for e in range(SIDE):
                for d in range(SIDE):
                    ex, ey = (e, d) if axis == 0 else (d, e)
                    base = slots_of(ex, ey)
                    if d == 2:
                        z[base : base + SLOTS] = jnp.zeros((SLOTS, *z.shape[1:]), z.dtype)
                    elif d:
                        source = sent[axis * 2 + (3 - d) // 2].at[pl.ds(e * SLOTS, SLOTS)]
                        pltpu.make_async_copy(source, z.at[pl.ds(base, SLOTS)], sem).start()
                    else:
                        holder = device_at(x, y, ex, ey)
                        for s in range(SLOTS):
                            local = table_ref[(me * SIDE * SIDE + holder) * SLOTS + s]
                            start_block(held[axis * SIDE + e], local, z.at[base + s], sem)
        for z in (zlo, zhi):
            for k in range(SIDE * (SIDE - 1)):
                part = z.at[pl.ds(k * SLOTS, SLOTS)]
                pltpu.make_async_copy(held[0][0], part, sem).wait()

    @pl.loop(0, SIDE * SIDE * SLOTS)
    def _(k):
        use_ref[r * SIDE * SIDE * SLOTS + k] = -1

    total = None
    for t in range(NZ):
        slot = slot_at(t)
        use_ref[r * SIDE * SIDE * SLOTS + slot] = t
        z = jnp.concatenate([zlo[slot], zhi[slot]], axis=1)
        term = lax.dot_general(z, f_ref[0, t], NT, preferred_element_type=jnp.float32)
        total = term if total is None else total + term
    acc_ref[0] = total
    buses = lax.broadcasted_iota(jnp.int32, (BUSES, BLK), 0)
    onehot_ref[...] = jnp.where(buses == bus_ref[0], 1.0, 0.0).astype(jnp.bfloat16)


def early(scalars, arrays, factor, bus):
    width = arrays[0].shape[1]
    slots = SIDE * SIDE * SLOTS
    grid_spec = pltpu.PrefetchScalarGridSpec(
        num_scalar_prefetch=len(scalars),
        grid=(RB_DEV,),
        in_specs=[ANY] * len(arrays)
        + [
            pl.BlockSpec((1, NZ, BLK, BLK), lambda r, *_: (r, 0, 0, 0)),
            pl.BlockSpec((1, 1, BLK), lambda r, *_: (r, 0, 0)),
        ],
        out_specs=[
            pl.BlockSpec((1, width, BLK), lambda r, *_: (r, 0, 0)),
            pl.BlockSpec(memory_space=pltpu.SMEM),
            pl.BlockSpec((BUSES, BLK), lambda r, *_: (0, r)),
        ],
        scratch_shapes=[
            pltpu.VMEM((slots, width, HALF), jnp.bfloat16),
            pltpu.VMEM((slots, width, HALF), jnp.bfloat16),
            pltpu.SemaphoreType.DMA,
        ],
    )
    return pl.pallas_call(
        early_kernel,
        grid_spec=grid_spec,
        out_shape=[
            jax.ShapeDtypeStruct((RB_DEV, width, BLK), jnp.float32),
            jax.ShapeDtypeStruct((RB_DEV * slots,), jnp.int32),
            jax.ShapeDtypeStruct((BUSES, RB_DEV * BLK), jnp.bfloat16),
        ],
        compiler_params=pltpu.CompilerParams(vmem_limit_bytes=ALL_VMEM),
        cost_estimate=pl.CostEstimate(
            flops=2 * RB_DEV * NZ * BLK * BLK * width, bytes_accessed=36 << 20, transcendentals=0
        ),
    )(*scalars, *arrays, factor, bus)


def late_kernel(use_ref, lo_ref, hi_ref, f_ref, acc_ref, temporal_ref, cap_ref, spr_ref, onehot_ref, *refs):
    out_ref, onehot, injected, sem = refs
    r = pl.program_id(0)
    base = r * SIDE * SIDE * SLOTS

    @pl.when(r == 0)
    def _():
        pltpu.make_async_copy(onehot_ref, onehot, sem).start()

    def piece(slot, half):
        t = use_ref[base + slot]
        f = f_ref[0, jnp.maximum(t, 0), :, half * HALF : (half + 1) * HALF]
        return jnp.where(t >= 0, f, jnp.zeros_like(f))

    total = acc_ref[0]
    for e in range(SIDE):
        for s in range(SLOTS):
            z = jnp.concatenate([lo_ref[e * SLOTS + s], hi_ref[e * SLOTS + s]], axis=1)
            f = jnp.concatenate(
                [piece(slots_of(e, 2) + s, 0), piece(slots_of(2, e) + s, 1)], axis=1
            )
            total += lax.dot_general(z, f, NT, preferred_element_type=jnp.float32)
    cap, spr = cap_ref[0], spr_ref[0]
    parts = []
    for s in range(total.shape[0] // HOURS):
        spatial = total[s * HOURS : (s + 1) * HOURS].astype(jnp.bfloat16)
        weather = jnp.dot(temporal_ref[...], spatial, preferred_element_type=jnp.float32)
        parts.append(cap * jnp.exp(spr * weather - 0.5 * spr * spr))
    injected[r] = jnp.concatenate(parts, axis=0).astype(jnp.bfloat16)

    @pl.when(r == pl.num_programs(0) - 1)
    def _():
        pltpu.make_async_copy(onehot_ref, onehot, sem).wait()
        rows = jnp.concatenate([injected[k] for k in range(RB_DEV)], axis=1)
        power = lax.dot_general(onehot[...], rows, NT, preferred_element_type=jnp.float32)
        out_ref[...] = power.astype(jnp.bfloat16)


def late(use, opposite, factor, acc, temporal, vectors, onehot):
    width = acc.shape[1]
    vec = pl.BlockSpec((1, 1, BLK), lambda r, *_: (r, 0, 0))
    grid_spec = pltpu.PrefetchScalarGridSpec(
        num_scalar_prefetch=1,
        grid=(RB_DEV,),
        in_specs=[
            pl.BlockSpec(opposite[0].shape, lambda r, *_: (0, 0, 0)),
            pl.BlockSpec(opposite[0].shape, lambda r, *_: (0, 0, 0)),
            pl.BlockSpec((1, NZ, BLK, BLK), lambda r, *_: (r, 0, 0, 0)),
            pl.BlockSpec((1, width, BLK), lambda r, *_: (r, 0, 0)),
            pl.BlockSpec((HOURS, HOURS), lambda r, *_: (0, 0)),
            vec,
            vec,
            ANY,
        ],
        out_specs=pl.BlockSpec((BUSES, width), lambda r, *_: (0, 0)),
        scratch_shapes=[
            pltpu.VMEM(onehot.shape, onehot.dtype),
            pltpu.VMEM((RB_DEV, width, BLK), jnp.bfloat16),
            pltpu.SemaphoreType.DMA,
        ],
    )
    return pl.pallas_call(
        late_kernel,
        grid_spec=grid_spec,
        out_shape=jax.ShapeDtypeStruct((BUSES, width), jnp.bfloat16),
        compiler_params=pltpu.CompilerParams(vmem_limit_bytes=ALL_VMEM),
        cost_estimate=pl.CostEstimate(
            flops=RB_DEV * NZ * BLK * BLK * width,
            bytes_accessed=28 << 20,
            transcendentals=RB_DEV * BLK * width,
        ),
    )(use, *opposite, factor, acc, temporal, *vectors, onehot)


def shards(normals, pattern, factor, temporal, capacity, spread, bus_map):
    n = SIDE
    sites = n * n
    me = lax.axis_index("site")
    portion = lax.all_gather(factor, "scen", axis=2, tiled=True)

    ids = jnp.arange(sites * CB_DEV, dtype=jnp.int32)
    wanted = pattern.reshape(sites, -1)
    needed = jnp.any(wanted[:, :, None] == ids[None, None, :], axis=1)
    needed = needed.reshape(sites, sites, CB_DEV).astype(jnp.int32)
    lower = (jnp.arange(CB_DEV)[:, None] < jnp.arange(CB_DEV)[None, :]).astype(jnp.int32)
    rank = jnp.sum(needed[:, :, :, None] * lower[None, None], axis=2)
    slot_ids = jnp.arange(SLOTS, dtype=jnp.int32)
    chosen = (needed[..., None] == 1) & (rank[..., None] == slot_ids)
    local_ids = jnp.arange(CB_DEV, dtype=jnp.int32)
    table = jnp.sum(jnp.where(chosen, local_ids[:, None], 0), axis=2)

    table = table.reshape(-1)
    index = me.reshape(1).astype(jnp.int32)

    parts = reblocked(normals.T)
    lines = [[tuple(parts[2 * axis : 2 * axis + 2]), None, None, None] for axis in (0, 1)]
    ring = [(axis, e) for axis in (0, 1) for e in (1, 3)]
    below = [step(lines[axis][0][0], axis, 1) for axis in (0, 1)]
    above = [step(lines[axis][0][1], axis, -1) for axis in (0, 1)]
    first = below + above
    for axis in (0, 1):
        own = lines[axis][0]
        lines[axis][3] = (below[axis], step(after(own[1], *first), axis, 1))
        lines[axis][1] = (step(after(own[0], *first), axis, -1), above[axis])
    for axis in (0, 1):
        lines[axis][2] = (step(after(below[axis], table), axis, 1), step(above[axis], axis, -1))
    tables = (index, table)
    out = picked((1, 3), (0, 1, 3), tables, lines)
    out = picked((1, 3), (2,), tables, lines, out)
    sent = [step(b, 1 - axis, d) for b, (axis, d) in zip(out, ring)]
    flat = (rank.reshape(-1), pattern.reshape(-1))
    held = RB_DEV * BLK
    bus = lax.dynamic_slice_in_dim(bus_map, me * held, held, 0)
    out = picked((2,), (0, 1, 2, 3), (after(index, out[0], *flat, bus), table), lines)
    opposite = [step(after(b, *sent), 1 - axis, 2) for axis, b in enumerate(out)]
    arrays = [p for line in lines for pair in line for p in pair] + sent
    shape = (RB_DEV, 1, BLK)
    scalars = (index, table, *flat)
    vectors = (capacity.reshape(shape), spread.reshape(shape))
    acc, use, onehot = early(scalars, arrays, portion, bus.reshape(shape))
    power = late(use, opposite, portion, acc, temporal, vectors, onehot)
    tiles = lax.all_to_all(power.reshape(sites, -1, power.shape[1]), "site", 0, 0, tiled=True)
    return jnp.sum(tiles.astype(jnp.float32), axis=0)


def solution(mesh):
    placed = (P("site", "scen"), P(), P("site", None, "scen", None), P(), P("site"), P("site"), P())
    return jax.shard_map(
        shards, mesh=mesh, in_specs=placed, out_specs=P("site", "scen"), check_vma=False
    )
```

```python
import functools

import jax
import jax.numpy as jnp
from jax import lax
from jax.experimental import pallas as pl
from jax.experimental.pallas import tpu as pltpu
from jax.sharding import PartitionSpec as P

BLK = 256
HALF = 128
HOURS = 168
NZ = 40
SLOTS = 5
FEW = 5
RB_DEV = 4
CB_DEV = 10
SIDE = 4
BUSES = 1024
COLS = 160
ALL_VMEM = 60 << 20


def shift(value, dx, dy):
    n = SIDE
    pairs = [
        (x * n + y, ((x + dx) % n) * n + (y + dy) % n) for x in range(n) for y in range(n)
    ]
    return lax.ppermute(value, "site", pairs)


def step(value, axis, d):
    return shift(value, d, 0) if axis == 0 else shift(value, 0, d)


def after(value, *others):
    return lax.optimization_barrier((value, *others))[0]


VMEM = pl.BlockSpec(memory_space=pltpu.VMEM)


def reblock_kernel(z_ref, *outs):
    for b in range(CB_DEV):
        for h in range(2):
            start = b * BLK + h * HALF
            outs[h * 2 + b // FEW][b % FEW] = z_ref[:, start : start + HALF]


def reblocked(normals_t):
    width = normals_t.shape[0]
    out = jax.ShapeDtypeStruct((FEW, width, HALF), normals_t.dtype)
    return pl.pallas_call(
        reblock_kernel,
        in_specs=[VMEM],
        out_specs=[VMEM] * 4,
        out_shape=[out] * 4,
        compiler_params=pltpu.CompilerParams(vmem_limit_bytes=ALL_VMEM),
    )(normals_t)


ANY = pl.BlockSpec(memory_space=pl.ANY)


def start_block(pair, local, target, sem):
    @pl.when(local < FEW)
    def _():
        pltpu.make_async_copy(pair[0].at[jnp.minimum(local, FEW - 1)], target, sem).start()

    @pl.when(local >= FEW)
    def _():
        pltpu.make_async_copy(pair[1].at[jnp.maximum(local - FEW, 0)], target, sem).start()


def wait_block(pair, target, sem):
    pltpu.make_async_copy(pair[0].at[0], target, sem).wait()


def pairs(refs):
    return [refs[k : k + 2] for k in range(0, len(refs), 2)]


def device_at(x, y, ex, ey):
    return lax.rem(x + ex, SIDE) * SIDE + lax.rem(y + ey, SIDE)


def pick_kernel(hops, holders, aliased, me_ref, table_ref, *refs):
    span, count = len(holders), 2 * len(hops)
    held = pairs(refs[: 4 * span])
    refs = refs[4 * span + aliased * count :]
    outs, buffers, came, gone = refs[:count], *refs[count:]
    x, y = me_ref[0] // SIDE, lax.rem(me_ref[0], SIDE)
    for k in range(count):
        axis, d = k // len(hops), hops[k % len(hops)]
        user = device_at(x, y, 0, d) if axis == 0 else device_at(x, y, d, 0)
        for i, e in enumerate(holders):
            holder = device_at(x, y, e, 0) if axis == 0 else device_at(x, y, 0, e)
            for s in range(SLOTS):
                local = table_ref[(user * SIDE * SIDE + holder) * SLOTS + s]
                start_block(held[axis * span + i], local, buffers.at[k, i, s], came.at[k])
    for k in range(count):
        for i in range(span):
            pltpu.make_async_copy(held[0][0], buffers.at[k, i], came.at[k]).wait()
        for i, e in enumerate(holders):
            target = outs[k].at[pl.ds(e * SLOTS, SLOTS)]
            pltpu.make_async_copy(buffers.at[k, i], target, gone.at[k, i]).start()
    for k in range(count):
        for i, e in enumerate(holders):
            target = outs[k].at[pl.ds(e * SLOTS, SLOTS)]
            pltpu.make_async_copy(buffers.at[k, i], target, gone.at[k, i]).wait()


def picked(hops, holders, scalars, lines, begun=()):
    width = lines[0][0][0].shape[1]
    out = jax.ShapeDtypeStruct((SIDE * SLOTS, width, HALF), jnp.bfloat16)
    outs, span = 2 * len(hops), len(holders)
    held = [p for line in lines for e in holders for p in line[e]]
    return pl.pallas_call(
        functools.partial(pick_kernel, hops, holders, bool(begun)),
        grid_spec=pltpu.PrefetchScalarGridSpec(
            num_scalar_prefetch=2,
            grid=(),
            in_specs=[ANY] * (len(held) + len(begun)),
            out_specs=[ANY] * outs,
            scratch_shapes=[
                pltpu.VMEM((outs, span, SLOTS, width, HALF), out.dtype),
                pltpu.SemaphoreType.DMA((outs,)),
                pltpu.SemaphoreType.DMA((outs, span)),
            ],
        ),
        out_shape=[out] * outs,
        input_output_aliases={2 + len(held) + k: k for k in range(len(begun))},
        compiler_params=pltpu.CompilerParams(vmem_limit_bytes=ALL_VMEM),
    )(*scalars, *held, *begun)


def slots_of(ex, ey):
    return (ex * SIDE + ey) * SLOTS


NT = (((1,), (1,)), ((), ()))


def early_kernel(me_ref, table_ref, rank_ref, cols_ref, *refs):
    held, sent, f_ref, acc_ref, use_ref, zlo, zhi, sem = (
        pairs(refs[:16]), refs[16:20], *refs[20:]
    )
    r = pl.program_id(0)
    me = me_ref[0]
    x, y = me // SIDE, lax.rem(me, SIDE)

    def slot_at(t):
        col = cols_ref[(me * RB_DEV + r) * NZ + t]
        holder = col // CB_DEV
        ex = lax.rem(holder // SIDE - x + SIDE, SIDE)
        ey = lax.rem(lax.rem(holder, SIDE) - y + SIDE, SIDE)
        return slots_of(ex, ey) + rank_ref[me * COLS + col]

    @pl.when(r == 0)
    def _():
        for axis, z in ((0, zlo), (1, zhi)):
            for e in range(SIDE):
                for d in range(SIDE):
                    ex, ey = (e, d) if axis == 0 else (d, e)
                    base = slots_of(ex, ey)
                    if d == 2:
                        z[base : base + SLOTS] = jnp.zeros((SLOTS, *z.shape[1:]), z.dtype)
                    elif d:
                        source = sent[axis * 2 + (3 - d) // 2].at[pl.ds(e * SLOTS, SLOTS)]
                        pltpu.make_async_copy(source, z.at[pl.ds(base, SLOTS)], sem).start()
                    else:
                        holder = device_at(x, y, ex, ey)
                        for s in range(SLOTS):
                            local = table_ref[(me * SIDE * SIDE + holder) * SLOTS + s]
                            start_block(held[axis * SIDE + e], local, z.at[base + s], sem)
        for z in (zlo, zhi):
            for k in range(SIDE * (SIDE - 1)):
                part = z.at[pl.ds(k * SLOTS, SLOTS)]
                pltpu.make_async_copy(held[0][0], part, sem).wait()

    @pl.loop(0, SIDE * SIDE * SLOTS)
    def _(k):
        use_ref[r * SIDE * SIDE * SLOTS + k] = -1

    total = None
    for t in range(NZ):
        slot = slot_at(t)
        use_ref[r * SIDE * SIDE * SLOTS + slot] = t
        z = jnp.concatenate([zlo[slot], zhi[slot]], axis=1)
        term = lax.dot_general(z, f_ref[0, t], NT, preferred_element_type=jnp.float32)
        total = term if total is None else total + term
    acc_ref[0] = total


def onehot_kernel(bus_ref, onehot_ref):
    buses = lax.broadcasted_iota(jnp.int32, (BUSES, BLK), 0)
    onehot_ref[...] = jnp.where(buses == bus_ref[0], 1.0, 0.0).astype(jnp.bfloat16)


def onehot_of(bus):
    return pl.pallas_call(
        onehot_kernel,
        grid=(RB_DEV,),
        in_specs=[pl.BlockSpec((1, 1, BLK), lambda r: (r, 0, 0))],
        out_specs=pl.BlockSpec((BUSES, BLK), lambda r: (0, r)),
        out_shape=jax.ShapeDtypeStruct((BUSES, RB_DEV * BLK), jnp.bfloat16),
    )(bus)


def early(scalars, arrays, factor):
    width = arrays[0].shape[1]
    slots = SIDE * SIDE * SLOTS
    grid_spec = pltpu.PrefetchScalarGridSpec(
        num_scalar_prefetch=len(scalars),
        grid=(RB_DEV,),
        in_specs=[ANY] * len(arrays)
        + [
            pl.BlockSpec((1, NZ, BLK, BLK), lambda r, *_: (r, 0, 0, 0)),
        ],
        out_specs=[
            pl.BlockSpec((1, width, BLK), lambda r, *_: (r, 0, 0)),
            pl.BlockSpec(memory_space=pltpu.SMEM),
        ],
        scratch_shapes=[
            pltpu.VMEM((slots, width, HALF), jnp.bfloat16),
            pltpu.VMEM((slots, width, HALF), jnp.bfloat16),
            pltpu.SemaphoreType.DMA,
        ],
    )
    return pl.pallas_call(
        early_kernel,
        grid_spec=grid_spec,
        out_shape=[
            jax.ShapeDtypeStruct((RB_DEV, width, BLK), jnp.float32),
            jax.ShapeDtypeStruct((RB_DEV * slots,), jnp.int32),
        ],
        compiler_params=pltpu.CompilerParams(vmem_limit_bytes=ALL_VMEM),
        cost_estimate=pl.CostEstimate(
            flops=2 * RB_DEV * NZ * BLK * BLK * width, bytes_accessed=36 << 20, transcendentals=0
        ),
    )(*scalars, *arrays, factor)


def late_kernel(use_ref, lo_ref, hi_ref, f_ref, acc_ref, temporal_ref, cap_ref, spr_ref, onehot_ref, *refs):
    out_ref, onehot, injected, sem = refs
    r = pl.program_id(0)
    base = r * SIDE * SIDE * SLOTS

    @pl.when(r == 0)
    def _():
        pltpu.make_async_copy(onehot_ref, onehot, sem).start()

    def piece(slot, half):
        t = use_ref[base + slot]
        f = f_ref[0, jnp.maximum(t, 0), :, half * HALF : (half + 1) * HALF]
        return jnp.where(t >= 0, f, jnp.zeros_like(f))

    total = acc_ref[0]
    for e in range(SIDE):
        for s in range(SLOTS):
            z = jnp.concatenate([lo_ref[e * SLOTS + s], hi_ref[e * SLOTS + s]], axis=1)
            f = jnp.concatenate(
                [piece(slots_of(e, 2) + s, 0), piece(slots_of(2, e) + s, 1)], axis=1
            )
            total += lax.dot_general(z, f, NT, preferred_element_type=jnp.float32)
    cap, spr = cap_ref[0], spr_ref[0]
    parts = []
    for s in range(total.shape[0] // HOURS):
        spatial = total[s * HOURS : (s + 1) * HOURS].astype(jnp.bfloat16)
        weather = jnp.dot(temporal_ref[...], spatial, preferred_element_type=jnp.float32)
        parts.append(cap * jnp.exp(spr * weather - 0.5 * spr * spr))
    injected[r] = jnp.concatenate(parts, axis=0).astype(jnp.bfloat16)

    @pl.when(r == pl.num_programs(0) - 1)
    def _():
        pltpu.make_async_copy(onehot_ref, onehot, sem).wait()
        rows = jnp.concatenate([injected[k] for k in range(RB_DEV)], axis=1)
        power = lax.dot_general(onehot[...], rows, NT, preferred_element_type=jnp.float32)
        out_ref[...] = power.astype(jnp.bfloat16)


def late(use, opposite, factor, acc, temporal, vectors, onehot):
    width = acc.shape[1]
    vec = pl.BlockSpec((1, 1, BLK), lambda r, *_: (r, 0, 0))
    grid_spec = pltpu.PrefetchScalarGridSpec(
        num_scalar_prefetch=1,
        grid=(RB_DEV,),
        in_specs=[
            pl.BlockSpec(opposite[0].shape, lambda r, *_: (0, 0, 0)),
            pl.BlockSpec(opposite[0].shape, lambda r, *_: (0, 0, 0)),
            pl.BlockSpec((1, NZ, BLK, BLK), lambda r, *_: (r, 0, 0, 0)),
            pl.BlockSpec((1, width, BLK), lambda r, *_: (r, 0, 0)),
            pl.BlockSpec((HOURS, HOURS), lambda r, *_: (0, 0)),
            vec,
            vec,
            ANY,
        ],
        out_specs=pl.BlockSpec((BUSES, width), lambda r, *_: (0, 0)),
        scratch_shapes=[
            pltpu.VMEM(onehot.shape, onehot.dtype),
            pltpu.VMEM((RB_DEV, width, BLK), jnp.bfloat16),
            pltpu.SemaphoreType.DMA,
        ],
    )
    return pl.pallas_call(
        late_kernel,
        grid_spec=grid_spec,
        out_shape=jax.ShapeDtypeStruct((BUSES, width), jnp.bfloat16),
        compiler_params=pltpu.CompilerParams(vmem_limit_bytes=ALL_VMEM),
        cost_estimate=pl.CostEstimate(
            flops=RB_DEV * NZ * BLK * BLK * width,
            bytes_accessed=28 << 20,
            transcendentals=RB_DEV * BLK * width,
        ),
    )(use, *opposite, factor, acc, temporal, *vectors, onehot)


def shards(normals, pattern, factor, temporal, capacity, spread, bus_map):
    n = SIDE
    sites = n * n
    me = lax.axis_index("site")
    portion = lax.all_gather(factor, "scen", axis=2, tiled=True)

    ids = jnp.arange(sites * CB_DEV, dtype=jnp.int32)
    wanted = pattern.reshape(sites, -1)
    needed = jnp.any(wanted[:, :, None] == ids[None, None, :], axis=1)
    needed = needed.reshape(sites, sites, CB_DEV).astype(jnp.int32)
    lower = (jnp.arange(CB_DEV)[:, None] < jnp.arange(CB_DEV)[None, :]).astype(jnp.int32)
    rank = jnp.sum(needed[:, :, :, None] * lower[None, None], axis=2)
    slot_ids = jnp.arange(SLOTS, dtype=jnp.int32)
    chosen = (needed[..., None] == 1) & (rank[..., None] == slot_ids)
    local_ids = jnp.arange(CB_DEV, dtype=jnp.int32)
    table = jnp.sum(jnp.where(chosen, local_ids[:, None], 0), axis=2)

    table = table.reshape(-1)
    index = me.reshape(1).astype(jnp.int32)

    parts = reblocked(normals.T)
    lines = [[tuple(parts[2 * axis : 2 * axis + 2]), None, None, None] for axis in (0, 1)]
    ring = [(axis, e) for axis in (0, 1) for e in (1, 3)]
    below = [step(lines[axis][0][0], axis, 1) for axis in (0, 1)]
    above = [step(lines[axis][0][1], axis, -1) for axis in (0, 1)]
    first = below + above
    for axis in (0, 1):
        own = lines[axis][0]
        lines[axis][3] = (below[axis], step(after(own[1], *first), axis, 1))
        lines[axis][1] = (step(after(own[0], *first), axis, -1), above[axis])
    for axis in (0, 1):
        lines[axis][2] = (step(after(below[axis], table), axis, 1), step(above[axis], axis, -1))
    tables = (index, table)
    out = picked((1, 3), (0, 1, 3), tables, lines)
    out = picked((1, 3), (2,), tables, lines, out)
    sent = [step(b, 1 - axis, d) for b, (axis, d) in zip(out, ring)]
    flat = (rank.reshape(-1), pattern.reshape(-1))
    held = RB_DEV * BLK
    bus = lax.dynamic_slice_in_dim(bus_map, me * held, held, 0)
    onehot = onehot_of(bus.reshape(RB_DEV, 1, BLK))
    out = picked((2,), (0, 1, 2, 3), (after(index, out[0], *flat, onehot), table), lines)
    opposite = [step(after(b, *sent), 1 - axis, 2) for axis, b in enumerate(out)]
    arrays = [p for line in lines for pair in line for p in pair] + sent
    shape = (RB_DEV, 1, BLK)
    scalars = (index, table, *flat)
    vectors = (capacity.reshape(shape), spread.reshape(shape))
    acc, use = early(scalars, arrays, portion)
    power = late(use, opposite, portion, acc, temporal, vectors, onehot)
    tiles = lax.all_to_all(power.reshape(sites, -1, power.shape[1]), "site", 0, 0, tiled=True)
    return jnp.sum(tiles.astype(jnp.float32), axis=0)


def solution(mesh):
    placed = (P("site", "scen"), P(), P("site", None, "scen", None), P(), P("site"), P("site"), P())
    return jax.shard_map(
        shards, mesh=mesh, in_specs=placed, out_specs=P("site", "scen"), check_vma=False
    )
```
